32 devices in a mesh: gx: 4 (over z), gy: 4 (over y, x), gz: 2 (over core).
Axes of the slice: x: 2, y: 2, z: 4, core: 2. Of those that a mesh axis runs over, the one named last changes fastest.
Arguments:
- links: bfloat16 [4, 4, 16, 2, 9, 64, 128], P('gx', 'gy', 'gz'), may hold values from -0.5 to 0.5
- null_vectors: bfloat16 [4, 4, 16, 2, 32, 128], P('gx', 'gy', 'gz'), may hold values from -1.796875 to 1.796875
- offsets: int32 [9, 4], replicated, may hold values from -1 to 1, as said below
- place: int32 [2, 2, 8, 1], replicated, may hold values from 0 to 7, as said below
Outputs:
- coarse_links: float32 [4, 2, 4, 9, 2048], P('gx', 'gz')
The draws below stay inside these ranges and needn't reach their ends.
Inputs may be any that keep to these rules, and one draw needn't show every extreme that they name: The rows are the nine offsets zero, plus one and minus one along each of x, y, z, t, each once, in some order. `place`: for each cx and each aligned run of 4 values of cz, the values over all cy, those cz and all ct are each of 0 to 7 once.
All inputs are finite; a program needn't handle non-finite values.
Results may differ from the reference program's by a relative error of at most 0.0029.
Values may be sent and summed in bfloat16 or wider, within the bound.
A program may use at most 64 MiB of HBM per device.

```python
import jax
import jax.numpy as jnp
from jax import lax

NC = 64
NV = 32
ZL = 8
TL = 2
NX = 4
NY = 4
NZ = 16
CX = 2
CY = 2
CZ = 8
CT = 1
CAP = 4
N_GX = 4
N_GZ = 2


STENCIL = ((0, 0, 0, 0), (1, 0, 0, 0), (-1, 0, 0, 0), (0, 1, 0, 0), (0, -1, 0, 0), (0, 0, 1, 0), (0, 0, -1, 0), (0, 0, 0, 1), (0, 0, 0, -1))


def draw_offsets(key, part):
    standard_table = jnp.array(STENCIL, jnp.int32)
    return jax.random.permutation(jax.random.fold_in(key, 11), standard_table).astype(jnp.int32)


def draw_place(key, part):
    block_count = CZ // (ZL // 2)
    line_size = CY * (ZL // 2) * CT
    key_list = jax.random.split(jax.random.fold_in(key, 23), CX * block_count)
    permuted = jax.vmap(lambda single: jax.random.permutation(single, line_size))(key_list)
    permuted = permuted.reshape(CX, block_count, CY, ZL // 2, CT)
    permuted = jnp.transpose(permuted, (0, 2, 1, 3, 4)).reshape(CX, CY, CZ, CT)
    return permuted.astype(jnp.int32)


def steps_of(own_key, extent, pieces, least, high):
    gain, own = 1.0, jax.random.fold_in(own_key, 6)
    for position, parts in pieces:
        draws = jnp.exp(jax.random.uniform(jax.random.fold_in(own, position), (parts,), jnp.float32, least / len(pieces), high / len(pieces)))
        gain = gain * jnp.repeat(draws, extent[position] // parts).reshape([-1 if axis == position else 1 for axis in range(len(extent))])
    return gain


def bell_draw(key, extent, deviation, limit, cuts=(), held_as=jnp.bfloat16):
    drawn = deviation * jax.random.normal(key, extent, jnp.float32)
    if cuts:
        drawn = drawn * steps_of(key, extent, cuts, -0.22, 0.18)
    return jnp.clip(drawn, -limit, limit).astype(held_as)


def setup_inputs(seed: int = 0) -> dict:
    splits = jax.random.split(jax.random.key(seed), 5)
    return {
        "links": bell_draw(splits[0], (NX, NY, NZ, TL, 9, NC, 2 * NC), (2 * NC) ** -0.5, 0.5, ((0, 4), (1, 4), (2, 2))),
        "null_vectors": bell_draw(splits[1], (NX, NY, NZ, TL, NV, 2 * NC), 0.3, 1.796875, ((0, 4), (1, 4), (2, 2))),
        "offsets": draw_offsets(jax.random.fold_in(splits[4], 71), 0),
        "place": draw_place(jax.random.fold_in(splits[4], 71), 0),
    }


def neighbour_blocks(neighbour):
    half_width = neighbour.shape[-1] // 2
    real_part = neighbour[..., :half_width]
    imag_part = neighbour[..., half_width:]
    upper_rows = jnp.concatenate([real_part, -imag_part], -1)
    lower_rows = jnp.concatenate([imag_part, real_part], -1)
    return jnp.concatenate([upper_rows, lower_rows], -2)


def conj_blocks(hopped):
    half_width = hopped.shape[-1] // 2
    hop_real = hopped[..., :half_width]
    hop_imag = hopped[..., half_width:]
    return jnp.concatenate([hopped, jnp.concatenate([hop_imag, -hop_real], -1)], -2)


def reference(links, null_vectors, offsets, place):
    x_count = links.shape[0]
    y_count = links.shape[1]
    z_count = links.shape[2]
    t_count = links.shape[3]
    vec_count = null_vectors.shape[4]
    flat_width = 2 * vec_count * vec_count
    y_parity = (jnp.arange(y_count, dtype=jnp.int32) % 2) * 2 - 1
    z_parity = (jnp.arange(z_count, dtype=jnp.int32) % 2) * 2 - 1
    t_parity = (jnp.arange(t_count, dtype=jnp.int32) % 2) * 2 - 1
    is_self = jnp.all(offsets == 0, axis=1).astype(jnp.float32)

    def one_slice(x_index):
        link_slice = lax.dynamic_index_in_dim(links, x_index, 0, False).astype(jnp.float32)
        own_vectors = lax.dynamic_index_in_dim(null_vectors, x_index, 0, False).astype(jnp.float32)
        x_sign = (x_index % 2) * 2 - 1
        term_list = []
        outside_list = []
        for direction in range(9):
            offset_row = offsets[direction]
            source = ((x_index + offset_row[0]) % x_count).astype(jnp.int32)
            neighbour = lax.dynamic_index_in_dim(null_vectors, source, 0, False)
            neighbour = jnp.roll(neighbour, -offset_row[1], axis=0)
            neighbour = jnp.roll(neighbour, -offset_row[2], axis=1)
            neighbour = jnp.roll(neighbour, -offset_row[3], axis=2)
            hopped = jnp.einsum('yztrc,yztuc->yztru', link_slice[:, :, :, direction],
                                neighbour_blocks(neighbour).astype(jnp.float32))
            hopped = lax.optimization_barrier(hopped.astype(jnp.bfloat16)).astype(jnp.float32)
            term = jnp.einsum('yztvq,yztqu->yztvu', own_vectors, conj_blocks(hopped))
            outside = ((offset_row[0] == x_sign).astype(jnp.float32)
                       + (offset_row[1] == y_parity).astype(jnp.float32)[:, None, None]
                       + (offset_row[2] == z_parity).astype(jnp.float32)[None, :, None]
                       + (offset_row[3] == t_parity).astype(jnp.float32)[None, None, :])
            term_list.append(term)
            outside_list.append(outside)
        spilled = jnp.zeros_like(term_list[0])
        for direction in range(9):
            spilled = spilled + (1.0 - outside_list[direction])[..., None, None] * term_list[direction]
        contrib = []
        for direction in range(9):
            contrib.append(outside_list[direction][..., None, None] * term_list[direction]
                           + is_self[direction] * spilled)
        stacked = jnp.stack(contrib)
        stacked = stacked.reshape(9, y_count // 2, 2, z_count // 2, 2, t_count // 2, 2, vec_count, 2 * vec_count)
        return stacked.sum(axis=(2, 4, 6))

    per_x = lax.map(one_slice, jnp.arange(x_count, dtype=jnp.int32))
    coarse = per_x.reshape((x_count // 2, 2) + per_x.shape[1:]).sum(axis=1)
    coarse = jnp.transpose(coarse, (0, 2, 3, 4, 1, 5, 6)).reshape(CX, CY, CZ, CT, 9, flat_width)
    target_x = 2 * jnp.arange(CX, dtype=jnp.int32)[:, None, None, None] + place // CAP
    block_z = jnp.broadcast_to((jnp.arange(CZ, dtype=jnp.int32) // (ZL // 2))[None, None, :, None], place.shape)
    slot_index = place % CAP
    result = jnp.zeros((N_GX, N_GZ, CAP, 9, flat_width), jnp.float32)
    return result.at[target_x.astype(jnp.int32), block_z.astype(jnp.int32), slot_index.astype(jnp.int32)].set(coarse)
```

```python
import functools

import jax
import jax.numpy as jnp
from jax import lax
from jax.experimental import pallas as pl
from jax.experimental.pallas import tpu as pltpu
from jax.sharding import PartitionSpec as P

MESH = pl.DeviceIdType.MESH
F32 = jnp.float32
BF16 = jnp.bfloat16
ZT, ALL, PART = 4, 9, 7


def rotated(value):
    half = value.shape[-1] // 2
    return pltpu.roll(value, half, 1)


def right_blocks(vectors):
    value = vectors.astype(F32)
    half = value.shape[-1] // 2
    lane = lax.broadcasted_iota(jnp.int32, value.shape, 1)
    first = jnp.where(lane < half, value, -value)
    second = rotated(value)
    return jnp.concatenate([first, second, second, -first], 0).astype(BF16)


def hop(left, right):
    return lax.dot_general(
        left, right, (((1,), (1,)), ((), ())), preferred_element_type=F32
    ).astype(BF16)


def mm(left, right):
    return jnp.dot(left, right, preferred_element_type=F32)


def fold(product):
    rows = product.shape[0] // 4
    a, b, c, d = (product[i * rows : (i + 1) * rows] for i in range(4))
    lane = lax.broadcasted_iota(jnp.int32, a.shape, 1)
    return jnp.where(lane < a.shape[1] // 2, a + rotated(c), rotated(b) + d)


def kernel(
    sizes,
    links_hbm,
    vec_hbm,
    offsets_ref,
    place_ref,
    out_ref,
    links,
    vec,
    halo,
    halo_z,
    blocks,
    vec32,
    left,
    left_t,
    acc,
    own,
    sendbuf,
    arrived,
    gathered,
    flat,
    link_sem,
    vec_sem,
    hs_sem,
    hr_sem,
    zs_sem,
    zr_sem,
    rs_sem,
    rr_sem,
    gs_sem,
    gr_sem,
):
    n_gx, n_gy, n_gz = sizes
    z_len, t_len, n_vec = vec.shape[0], vec.shape[1], vec.shape[2]
    n_comp = links.shape[3]
    q_count = z_len // 2
    gx, gy, gz = lax.axis_index("gx"), lax.axis_index("gy"), lax.axis_index("gz")
    xb, yb = gx % 2, gy % 2
    x_out = (gx + 2 * xb - 1 + n_gx) % n_gx
    x_in = gx + 1 - 2 * xb
    y_out = (gy + 2 * yb - 1 + n_gy) % n_gy
    y_in = gy + 1 - 2 * yb
    z_up, z_down = (gz + 1) % n_gz, (gz + n_gz - 1) % n_gz

    peers = []
    for dx in range(2):
        for dy in range(n_gy):
            if dx or dy:
                peers.append((dx, dy, (gx + dx * (1 - 2 * xb), (gy + dy) % n_gy, gz)))

    barrier = pltpu.get_barrier_semaphore()
    for _, _, device in peers:
        pl.semaphore_signal(barrier, inc=1, device_id=device, device_id_type=MESH)
    for device in ((x_out, gy, gz), (gx, gy, z_up), (gx, gy, z_down)):
        pl.semaphore_signal(barrier, inc=1, device_id=device, device_id_type=MESH)

    vec_copy = pltpu.make_async_copy(vec_hbm.at[0, 0], vec, vec_sem)
    vec_copy.start()

    def square(d):
        return (xb + d % 2) % 2 + 2 * ((yb + d // 2) % 2)

    link_copy = pltpu.make_async_copy(links_hbm.at[0, 0], links, link_sem)
    link_copy.start()

    codes = [
        offsets_ref[0, k] + 3 * offsets_ref[1, k] + 9 * offsets_ref[2, k] + 27 * offsets_ref[3, k]
        for k in range(ALL)
    ]

    def position(code):
        found = jnp.int32(0)
        for k in range(1, ALL):
            found = jnp.where(codes[k] == code, k, found)
        return found

    x_sign, y_sign = 2 * xb - 1, 2 * yb - 1
    k_zero = position(0)
    k_zp, k_zm, k_tp, k_tm = position(9), position(-9), position(27), position(-27)
    k_dirs = (position(-x_sign), position(x_sign), position(-3 * y_sign), position(3 * y_sign))

    vec_copy.wait()
    pl.semaphore_wait(barrier, len(peers) + 3)

    up_copy = pltpu.make_async_remote_copy(
        src_ref=vec.at[z_len - 1],
        dst_ref=halo_z.at[0],
        send_sem=zs_sem.at[0],
        recv_sem=zr_sem.at[0],
        device_id=(gx, gy, z_up),
        device_id_type=MESH,
    )
    down_copy = pltpu.make_async_remote_copy(
        src_ref=vec.at[0],
        dst_ref=halo_z.at[1],
        send_sem=zs_sem.at[1],
        recv_sem=zr_sem.at[1],
        device_id=(gx, gy, z_down),
        device_id_type=MESH,
    )
    up_copy.start()
    down_copy.start()

    targets = ((x_in, gy, gz), (x_out, gy, gz), (gx, y_in, gz), (gx, y_out, gz))

    def halo_copy(direction, d):
        flip = 1 if direction < 2 else 2
        if flip == 1:
            q = (xb + 1 + d % 2) % 2 + 2 * ((yb + d // 2) % 2)
        else:
            q = (xb + d % 2) % 2 + 2 * ((yb + 1 + d // 2) % 2)
        rows = pl.ds(2 * q, 2)
        return pltpu.make_async_remote_copy(
            src_ref=vec.at[rows],
            dst_ref=halo.at[direction, rows],
            send_sem=hs_sem.at[direction, d],
            recv_sem=hr_sem.at[direction, d],
            device_id=targets[direction],
            device_id_type=MESH,
        )

    def halo_arrival(direction, d):
        rows = pl.ds(2 * square(d), 2)
        return pltpu.make_async_remote_copy(
            src_ref=vec.at[rows],
            dst_ref=halo.at[direction, rows],
            send_sem=hs_sem.at[direction, d],
            recv_sem=hr_sem.at[direction, d],
            device_id=targets[direction],
            device_id_type=MESH,
        )

    for d in (1, 2, 3, 0):
        for direction in range(4):
            halo_copy(direction, d).start()

    def prepare(z, carry):
        for t in range(t_len):
            blocks[z + 1, t] = right_blocks(vec[z, t])
            vec32[z, t] = vec[z, t].astype(F32)
        return carry

    lax.fori_loop(0, z_len, prepare, 0)

    def prepare_left(q, carry):
        def pieces(dz, t):
            return [vec32[2 * q + dz, t, pl.ds(s, n_vec // 2, stride=2), :] for s in range(2)]

        site = {(dz, t): pieces(dz, t) for dz in range(2) for t in range(2)}
        shape = site[0, 0][0].shape
        lane = lax.broadcasted_iota(jnp.int32, shape, 1)
        low = lane < n_comp

        def pair(one, two):
            real = [jnp.where(low, one[s], rotated(two[s])) for s in range(2)]
            imag = [jnp.where(low, rotated(one[s]), two[s]) for s in range(2)]
            return jnp.concatenate(real + imag, 0).astype(BF16)

        left[q, :, : 2 * n_comp] = pair(site[0, 0], site[0, 1])
        left[q, :, 2 * n_comp :] = pair(site[1, 0], site[1, 1])
        left_t[q, :, : 2 * n_comp] = pair(site[0, 0], site[1, 0])
        left_t[q, :, 2 * n_comp :] = pair(site[0, 1], site[1, 1])
        return carry

    lax.fori_loop(0, q_count, prepare_left, 0)

    up_copy.wait_recv()
    down_copy.wait_recv()
    for t in range(t_len):
        blocks[0, t] = right_blocks(halo_z[0, t])
        blocks[z_len + 1, t] = right_blocks(halo_z[1, t])

    def rs_copy(d, part):
        rows = pl.ds(0, ZT) if part == 0 else pl.ds(ZT, PART - ZT)
        dx, dy = d % 2, d // 2
        return pltpu.make_async_remote_copy(
            src_ref=sendbuf.at[d, rows],
            dst_ref=arrived.at[d, rows],
            send_sem=rs_sem.at[part, d],
            recv_sem=rr_sem.at[part, d],
            device_id=(gx + dx * (1 - 2 * xb), gy + dy * (1 - 2 * yb), gz),
            device_id_type=MESH,
        )

    def local_part(d, put):
        q = square(d)
        z0 = 2 * q
        zero, z_inner, z_outer, t_inner, t_outer = {}, {}, {}, {}, {}
        for dz in range(2):
            z = z0 + dz
            k_in, k_back = (k_zm, k_zp) if dz == 0 else (k_zp, k_zm)
            for t in range(2):
                lhs = jnp.concatenate(
                    [
                        links[z, t, k_zero],
                        links[z0 + 1 - dz, t, k_in],
                        links[z, 1 - t, k_tp],
                        links[z, 1 - t, k_tm],
                    ],
                    0,
                )
                res = hop(lhs, blocks[z + 1, t])
                rows = [res[i * n_comp : (i + 1) * n_comp] for i in range(4)]
                zero[dz, t] = rows[0]
                z_inner[1 - dz, t] = rows[1]
                t_inner[dz, 1 - t] = rows[2] if t == 1 else rows[3]
                t_outer[dz, 1 - t] = rows[3] if t == 1 else rows[2]
                edge = blocks[z0, t] if dz == 0 else blocks[z0 + 3, t]
                z_outer[dz, t] = hop(links[z, t, k_in], edge)
        order = ((0, 0), (0, 1), (1, 0), (1, 1))
        lq = left[q]
        lt = left_t[q]
        total = mm(lq, jnp.concatenate([zero[s] for s in order], 0))
        total = total + mm(lq, jnp.concatenate([z_inner[s] for s in order], 0))
        total = total + mm(lq, jnp.concatenate([t_inner[s] for s in order], 0))
        acc[q] = total
        half = 2 * n_comp
        put(0, fold(mm(lq[:, half:], jnp.concatenate([z_outer[1, 0], z_outer[1, 1]], 0))))
        put(1, fold(mm(lq[:, :half], jnp.concatenate([z_outer[0, 0], z_outer[0, 1]], 0))))
        put(2, fold(mm(lt[:, half:], jnp.concatenate([t_outer[0, 1], t_outer[1, 1]], 0))))
        put(3, fold(mm(lt[:, :half], jnp.concatenate([t_outer[0, 0], t_outer[1, 0]], 0))))

    def halo_part(d, put):
        q = square(d)
        z0 = 2 * q
        lq = left[q]
        sums = []
        for direction in range(4):
            halo_arrival(direction, d).wait_recv()
            rows = []
            for dz in range(2):
                for t in range(2):
                    rows.append(
                        hop(
                            links[z0 + dz, t, k_dirs[direction]],
                            right_blocks(halo[direction, z0 + dz, t]),
                        )
                    )
            sums.append(mm(lq, jnp.concatenate(rows, 0)))
        put(4, fold(acc[q] + sums[0] + sums[2]))
        put(5, fold(sums[1]))
        put(6, fold(sums[3]))

    def put_own(i, value):
        own[i] = value

    def local_step(d, carry):
        def put(i, value):
            sendbuf[d, i] = value.astype(BF16)

        local_part(d, put)
        rs_copy(d, 0).start()
        return carry

    def halo_step(d, carry):
        def put(i, value):
            sendbuf[d, i] = value.astype(BF16)

        halo_part(d, put)
        rs_copy(d, 1).start()
        return carry

    link_copy.wait()
    lax.fori_loop(1, 4, local_step, 0)
    local_part(0, put_own)
    lax.fori_loop(1, 4, halo_step, 0)

    mine = gy // 2 * q_count + square(0)

    def ag_copy(index, device, part):
        rows = pl.ds(0, ZT) if part == 0 else pl.ds(ZT, ALL - ZT)
        return pltpu.make_async_remote_copy(
            src_ref=gathered.at[mine, rows],
            dst_ref=gathered.at[mine, rows],
            send_sem=gs_sem.at[part, index],
            recv_sem=gr_sem.at[part, index],
            device_id=device,
            device_id_type=MESH,
        )

    def put_all(i, value):
        gathered[mine, i] = value.astype(BF16)

    def got(d, i):
        return arrived[d, i].astype(F32)

    for d in range(1, 4):
        rs_copy(d, 0).wait_recv()
    for i in range(ZT):
        put_all(i, own[i] + got(1, i) + got(2, i) + got(3, i))
    for index, (_, _, device) in enumerate(peers):
        ag_copy(index, device, 0).start()

    halo_part(0, put_own)

    for d in range(1, 4):
        rs_copy(d, 1).wait_recv()
    put_all(4, own[4] + got(1, 4) + got(2, 4) + got(3, 4))
    put_all(6 - xb, own[5] + got(2, 5))
    put_all(5 + xb, got(1, 5) + got(3, 5))
    put_all(8 - yb, own[6] + got(1, 6))
    put_all(7 + yb, got(2, 6) + got(3, 6))
    for index, (_, _, device) in enumerate(peers):
        ag_copy(index, device, 1).start()

    kinds = []
    for k in range(ALL):
        kind = jnp.int32(0)
        for i, code in enumerate((9, -9, 27, -27, 0, 1, -1, 3, -3)):
            if i:
                kind = jnp.where(codes[k] == code, i, kind)
        kinds.append(kind)
    capacity = out_ref.shape[3]
    cy_count = n_gy // 2

    up_copy.wait_send()
    down_copy.wait_send()
    for d in range(4):
        for direction in range(4):
            halo_copy(direction, d).wait_send()
    for d in range(1, 4):
        for part in range(2):
            rs_copy(d, part).wait_send()
    for part in range(2):
        for index, (_, _, device) in enumerate(peers):
            ag_copy(index, device, part).wait_recv()

    lines = n_vec // 2

    sources = []
    for slot in range(capacity):
        source = jnp.int32(0)
        for cy in range(cy_count):
            for q in range(q_count):
                here = place_ref[gx // 2, cy, 0, gz * q_count + q]
                source = jnp.where(here == xb * capacity + slot, cy * q_count + q, source)
        sources.append(source)
    for k in range(ALL):
        base = k * capacity * lines
        for slot in range(capacity):
            at = base + slot * lines
            flat[at : at + lines, :] = gathered[sources[slot], kinds[k]].astype(F32)
        for i in range(lines):
            out_ref[0, 0, k, :, 2 * n_comp * i : 2 * n_comp * (i + 1)] = flat[
                pl.ds(base + i, capacity, stride=lines), :
            ]
    for part in range(2):
        for index, (_, _, device) in enumerate(peers):
            ag_copy(index, device, part).wait_send()


def solution(mesh):
    n_gx, n_gy, n_gz = mesh.shape["gx"], mesh.shape["gy"], mesh.shape["gz"]

    def local(links, null_vectors, offsets, place):
        z_len, t_len, stencil, n_comp, width = links.shape[2:]
        n_vec = null_vectors.shape[4]
        q_count = z_len // 2
        aggregates = n_gy // 2 * q_count
        capacity = aggregates // 2
        peers = 2 * n_gy - 1
        lines = n_vec // 2
        dma = pltpu.SemaphoreType.DMA
        result = pl.pallas_call(
            functools.partial(kernel, (n_gx, n_gy, n_gz)),
            out_shape=jax.ShapeDtypeStruct((1, 1, stencil, capacity, 2 * n_vec * n_vec), F32),
            in_specs=[
                pl.BlockSpec(memory_space=pltpu.HBM),
                pl.BlockSpec(memory_space=pltpu.HBM),
                pl.BlockSpec(memory_space=pltpu.SMEM),
                pl.BlockSpec(memory_space=pltpu.SMEM),
            ],
            out_specs=pl.BlockSpec(memory_space=pltpu.VMEM),
            scratch_shapes=[
                pltpu.VMEM((z_len, t_len, stencil, n_comp, width), BF16),
                pltpu.VMEM((z_len, t_len, n_vec, width), BF16),
                pltpu.VMEM((4, z_len, t_len, n_vec, width), BF16),
                pltpu.VMEM((2, t_len, n_vec, width), BF16),
                pltpu.VMEM((z_len + 2, t_len, width, width), BF16),
                pltpu.VMEM((z_len, t_len, n_vec, width), F32),
                pltpu.VMEM((q_count, 2 * n_vec, 4 * n_comp), BF16),
                pltpu.VMEM((q_count, 2 * n_vec, 4 * n_comp), BF16),
                pltpu.VMEM((q_count, 2 * n_vec, width), F32),
                pltpu.VMEM((PART, lines, width), F32),
                pltpu.VMEM((4, PART, lines, width), BF16),
                pltpu.VMEM((4, PART, lines, width), BF16),
                pltpu.VMEM((aggregates, ALL, lines, width), BF16),
                pltpu.VMEM((ALL * capacity * lines, width), F32),
                dma,
                dma,
                dma((4, 4)),
                dma((4, 4)),
                dma((2,)),
                dma((2,)),
                dma((2, 4)),
                dma((2, 4)),
                dma((2, peers)),
                dma((2, peers)),
            ],
            compiler_params=pltpu.CompilerParams(
                collective_id=0, has_side_effects=True, vmem_limit_bytes=63 * 2**20
            ),
            cost_estimate=pl.CostEstimate(
                flops=2 * z_len * t_len * stencil * n_comp * width * 6 * n_vec,
                bytes_accessed=links.size * 2 + null_vectors.size * 2,
                transcendentals=0,
            ),
        )(links, null_vectors, offsets.T, place.swapaxes(2, 3))
        return result.swapaxes(2, 3)

    placed = (
        P("gx", "gy", "gz", None, None, None, None),
        P("gx", "gy", "gz", None, None, None),
        P(),
        P(),
    )
    return jax.shard_map(
        local,
        mesh=mesh,
        in_specs=placed,
        out_specs=P("gx", "gz", None, None, None),
        check_vma=False,
    )
```

```python
import functools

import jax
import jax.numpy as jnp
from jax import lax
from jax.experimental import pallas as pl
from jax.experimental.pallas import tpu as pltpu
from jax.sharding import PartitionSpec as P

MESH = pl.DeviceIdType.MESH
F32 = jnp.float32
BF16 = jnp.bfloat16
ZT, ALL, PART = 4, 9, 7


def rotated(value):
    half = value.shape[-1] // 2
    return pltpu.roll(value, half, 1)


def right_blocks(vectors):
    value = vectors.astype(F32)
    half = value.shape[-1] // 2
    lane = lax.broadcasted_iota(jnp.int32, value.shape, 1)
    first = jnp.where(lane < half, value, -value)
    second = rotated(value)
    return jnp.concatenate([first, second, second, -first], 0).astype(BF16)


def hop(left, right):
    return lax.dot_general(
        left, right, (((1,), (1,)), ((), ())), preferred_element_type=F32
    ).astype(BF16)


def mm(left, right):
    return jnp.dot(left, right, preferred_element_type=F32)


def fold(product):
    rows = product.shape[0] // 4
    a, b, c, d = (product[i * rows : (i + 1) * rows] for i in range(4))
    lane = lax.broadcasted_iota(jnp.int32, a.shape, 1)
    return jnp.where(lane < a.shape[1] // 2, a + rotated(c), rotated(b) + d)


def kernel(
    sizes,
    links_hbm,
    vec_hbm,
    offsets_ref,
    place_ref,
    out_ref,
    links,
    vec,
    halo,
    halo_z,
    blocks,
    vec32,
    left,
    left_t,
    acc,
    own,
    sendbuf,
    arrived,
    gathered,
    flat,
    link_sem,
    vec_sem,
    hs_sem,
    hr_sem,
    zs_sem,
    zr_sem,
    rs_sem,
    rr_sem,
    gs_sem,
    gr_sem,
):
    n_gx, n_gy, n_gz = sizes
    z_len, t_len, n_vec = vec.shape[0], vec.shape[1], vec.shape[2]
    n_comp = links.shape[3]
    q_count = z_len // 2
    gx, gy, gz = lax.axis_index("gx"), lax.axis_index("gy"), lax.axis_index("gz")
    xb, yb = gx % 2, gy % 2
    x_out = (gx + 2 * xb - 1 + n_gx) % n_gx
    x_in = gx + 1 - 2 * xb
    y_out = (gy + 2 * yb - 1 + n_gy) % n_gy
    y_in = gy + 1 - 2 * yb
    z_up, z_down = (gz + 1) % n_gz, (gz + n_gz - 1) % n_gz

    peers = []
    for dx in range(2):
        for dy in range(n_gy):
            if dx or dy:
                peers.append((dx, dy, (gx + dx * (1 - 2 * xb), (gy + dy) % n_gy, gz)))

    barrier = pltpu.get_barrier_semaphore()
    for _, _, device in peers:
        pl.semaphore_signal(barrier, inc=1, device_id=device, device_id_type=MESH)
    for device in ((x_out, gy, gz), (gx, gy, z_up), (gx, gy, z_down)):
        pl.semaphore_signal(barrier, inc=1, device_id=device, device_id_type=MESH)

    vec_copy = pltpu.make_async_copy(vec_hbm.at[0, 0], vec, vec_sem)
    vec_copy.start()

    def square(d):
        return (xb + d % 2) % 2 + 2 * ((yb + d // 2) % 2)

    link_copy = pltpu.make_async_copy(links_hbm.at[0, 0], links, link_sem)
    link_copy.start()

    codes = [
        offsets_ref[0, k] + 3 * offsets_ref[1, k] + 9 * offsets_ref[2, k] + 27 * offsets_ref[3, k]
        for k in range(ALL)
    ]

    def position(code):
        found = jnp.int32(0)
        for k in range(1, ALL):
            found = jnp.where(codes[k] == code, k, found)
        return found

    x_sign, y_sign = 2 * xb - 1, 2 * yb - 1
    k_zero = position(0)
    k_zp, k_zm, k_tp, k_tm = position(9), position(-9), position(27), position(-27)
    k_dirs = (position(-x_sign), position(x_sign), position(-3 * y_sign), position(3 * y_sign))

    vec_copy.wait()

    def prepare(z, carry):
        for t in range(t_len):
            blocks[z + 1, t] = right_blocks(vec[z, t])
            vec32[z, t] = vec[z, t].astype(F32)
        return carry

    lax.fori_loop(0, z_len, prepare, 0)

    def prepare_left(q, carry):
        def pieces(dz, t):
            return [vec32[2 * q + dz, t, pl.ds(s, n_vec // 2, stride=2), :] for s in range(2)]

        site = {(dz, t): pieces(dz, t) for dz in range(2) for t in range(2)}
        shape = site[0, 0][0].shape
        lane = lax.broadcasted_iota(jnp.int32, shape, 1)
        low = lane < n_comp

        def pair(one, two):
            real = [jnp.where(low, one[s], rotated(two[s])) for s in range(2)]
            imag = [jnp.where(low, rotated(one[s]), two[s]) for s in range(2)]
            return jnp.concatenate(real + imag, 0).astype(BF16)

        left[q, :, : 2 * n_comp] = pair(site[0, 0], site[0, 1])
        left[q, :, 2 * n_comp :] = pair(site[1, 0], site[1, 1])
        left_t[q, :, : 2 * n_comp] = pair(site[0, 0], site[1, 0])
        left_t[q, :, 2 * n_comp :] = pair(site[0, 1], site[1, 1])
        return carry

    lax.fori_loop(0, q_count, prepare_left, 0)

    pl.semaphore_wait(barrier, len(peers) + 3)

    up_copy = pltpu.make_async_remote_copy(
        src_ref=vec.at[z_len - 1],
        dst_ref=halo_z.at[0],
        send_sem=zs_sem.at[0],
        recv_sem=zr_sem.at[0],
        device_id=(gx, gy, z_up),
        device_id_type=MESH,
    )
    down_copy = pltpu.make_async_remote_copy(
        src_ref=vec.at[0],
        dst_ref=halo_z.at[1],
        send_sem=zs_sem.at[1],
        recv_sem=zr_sem.at[1],
        device_id=(gx, gy, z_down),
        device_id_type=MESH,
    )
    up_copy.start()
    down_copy.start()

    targets = ((x_in, gy, gz), (x_out, gy, gz), (gx, y_in, gz), (gx, y_out, gz))

    def halo_copy(direction, d):
        flip = 1 if direction < 2 else 2
        if flip == 1:
            q = (xb + 1 + d % 2) % 2 + 2 * ((yb + d // 2) % 2)
        else:
            q = (xb + d % 2) % 2 + 2 * ((yb + 1 + d // 2) % 2)
        rows = pl.ds(2 * q, 2)
        return pltpu.make_async_remote_copy(
            src_ref=vec.at[rows],
            dst_ref=halo.at[direction, rows],
            send_sem=hs_sem.at[direction, d],
            recv_sem=hr_sem.at[direction, d],
            device_id=targets[direction],
            device_id_type=MESH,
        )

    def halo_arrival(direction, d):
        rows = pl.ds(2 * square(d), 2)
        return pltpu.make_async_remote_copy(
            src_ref=vec.at[rows],
            dst_ref=halo.at[direction, rows],
            send_sem=hs_sem.at[direction, d],
            recv_sem=hr_sem.at[direction, d],
            device_id=targets[direction],
            device_id_type=MESH,
        )

    for d in (1, 2, 3, 0):
        for direction in range(4):
            halo_copy(direction, d).start()

    up_copy.wait_recv()
    down_copy.wait_recv()
    for t in range(t_len):
        blocks[0, t] = right_blocks(halo_z[0, t])
        blocks[z_len + 1, t] = right_blocks(halo_z[1, t])

    def rs_copy(d, part):
        rows = pl.ds(0, ZT) if part == 0 else pl.ds(ZT, PART - ZT)
        dx, dy = d % 2, d // 2
        return pltpu.make_async_remote_copy(
            src_ref=sendbuf.at[d, rows],
            dst_ref=arrived.at[d, rows],
            send_sem=rs_sem.at[part, d],
            recv_sem=rr_sem.at[part, d],
            device_id=(gx + dx * (1 - 2 * xb), gy + dy * (1 - 2 * yb), gz),
            device_id_type=MESH,
        )

    def local_part(d, put):
        q = square(d)
        z0 = 2 * q
        zero, z_inner, z_outer, t_inner, t_outer = {}, {}, {}, {}, {}
        for dz in range(2):
            z = z0 + dz
            k_in, k_back = (k_zm, k_zp) if dz == 0 else (k_zp, k_zm)
            for t in range(2):
                lhs = jnp.concatenate(
                    [
                        links[z, t, k_zero],
                        links[z0 + 1 - dz, t, k_in],
                        links[z, 1 - t, k_tp],
                        links[z, 1 - t, k_tm],
                    ],
                    0,
                )
                res = hop(lhs, blocks[z + 1, t])
                rows = [res[i * n_comp : (i + 1) * n_comp] for i in range(4)]
                zero[dz, t] = rows[0]
                z_inner[1 - dz, t] = rows[1]
                t_inner[dz, 1 - t] = rows[2] if t == 1 else rows[3]
                t_outer[dz, 1 - t] = rows[3] if t == 1 else rows[2]
                edge = blocks[z0, t] if dz == 0 else blocks[z0 + 3, t]
                z_outer[dz, t] = hop(links[z, t, k_in], edge)
        order = ((0, 0), (0, 1), (1, 0), (1, 1))
        lq = left[q]
        lt = left_t[q]
        total = mm(lq, jnp.concatenate([zero[s] for s in order], 0))
        total = total + mm(lq, jnp.concatenate([z_inner[s] for s in order], 0))
        total = total + mm(lq, jnp.concatenate([t_inner[s] for s in order], 0))
        acc[q] = total
        half = 2 * n_comp
        put(0, fold(mm(lq[:, half:], jnp.concatenate([z_outer[1, 0], z_outer[1, 1]], 0))))
        put(1, fold(mm(lq[:, :half], jnp.concatenate([z_outer[0, 0], z_outer[0, 1]], 0))))
        put(2, fold(mm(lt[:, half:], jnp.concatenate([t_outer[0, 1], t_outer[1, 1]], 0))))
        put(3, fold(mm(lt[:, :half], jnp.concatenate([t_outer[0, 0], t_outer[1, 0]], 0))))

    def halo_part(d, put):
        q = square(d)
        z0 = 2 * q
        lq = left[q]
        sums = []
        for direction in range(4):
            halo_arrival(direction, d).wait_recv()
            rows = []
            for dz in range(2):
                for t in range(2):
                    rows.append(
                        hop(
                            links[z0 + dz, t, k_dirs[direction]],
                            right_blocks(halo[direction, z0 + dz, t]),
                        )
                    )
            sums.append(mm(lq, jnp.concatenate(rows, 0)))
        put(4, fold(acc[q] + sums[0] + sums[2]))
        put(5, fold(sums[1]))
        put(6, fold(sums[3]))

    def put_own(i, value):
        own[i] = value

    def local_step(d, carry):
        def put(i, value):
            sendbuf[d, i] = value.astype(BF16)

        local_part(d, put)
        rs_copy(d, 0).start()
        return carry

    def halo_step(d, carry):
        def put(i, value):
            sendbuf[d, i] = value.astype(BF16)

        halo_part(d, put)
        rs_copy(d, 1).start()
        return carry

    link_copy.wait()
    lax.fori_loop(1, 4, local_step, 0)
    local_part(0, put_own)
    mine = gy // 2 * q_count + square(0)

    def ag_copy(index, device, part):
        rows = pl.ds(0, ZT) if part == 0 else pl.ds(ZT, ALL - ZT)
        return pltpu.make_async_remote_copy(
            src_ref=gathered.at[mine, rows],
            dst_ref=gathered.at[mine, rows],
            send_sem=gs_sem.at[part, index],
            recv_sem=gr_sem.at[part, index],
            device_id=device,
            device_id_type=MESH,
        )

    def put_all(i, value):
        gathered[mine, i] = value.astype(BF16)

    def got(d, i):
        return arrived[d, i].astype(F32)

    for d in range(1, 4):
        rs_copy(d, 0).wait_recv()
    for i in range(ZT):
        put_all(i, own[i] + got(1, i) + got(2, i) + got(3, i))
    for index, (_, _, device) in enumerate(peers):
        ag_copy(index, device, 0).start()

    lax.fori_loop(1, 4, halo_step, 0)

    halo_part(0, put_own)

    for d in range(1, 4):
        rs_copy(d, 1).wait_recv()
    put_all(4, own[4] + got(1, 4) + got(2, 4) + got(3, 4))
    put_all(6 - xb, own[5] + got(2, 5))
    put_all(5 + xb, got(1, 5) + got(3, 5))
    put_all(8 - yb, own[6] + got(1, 6))
    put_all(7 + yb, got(2, 6) + got(3, 6))
    for index, (_, _, device) in enumerate(peers):
        ag_copy(index, device, 1).start()

    kinds = []
    for k in range(ALL):
        kind = jnp.int32(0)
        for i, code in enumerate((9, -9, 27, -27, 0, 1, -1, 3, -3)):
            if i:
                kind = jnp.where(codes[k] == code, i, kind)
        kinds.append(kind)
    capacity = out_ref.shape[3]
    cy_count = n_gy // 2

    up_copy.wait_send()
    down_copy.wait_send()
    for d in range(4):
        for direction in range(4):
            halo_copy(direction, d).wait_send()
    for d in range(1, 4):
        for part in range(2):
            rs_copy(d, part).wait_send()
    for part in range(2):
        for index, (_, _, device) in enumerate(peers):
            ag_copy(index, device, part).wait_recv()

    lines = n_vec // 2

    sources = []
    for slot in range(capacity):
        source = jnp.int32(0)
        for cy in range(cy_count):
            for q in range(q_count):
                here = place_ref[gx // 2, cy, 0, gz * q_count + q]
                source = jnp.where(here == xb * capacity + slot, cy * q_count + q, source)
        sources.append(source)
    for k in range(ALL):
        base = k * capacity * lines
        for slot in range(capacity):
            at = base + slot * lines
            flat[at : at + lines, :] = gathered[sources[slot], kinds[k]].astype(F32)
        for i in range(lines):
            out_ref[0, 0, k, :, 2 * n_comp * i : 2 * n_comp * (i + 1)] = flat[
                pl.ds(base + i, capacity, stride=lines), :
            ].astype(BF16)
    for part in range(2):
        for index, (_, _, device) in enumerate(peers):
            ag_copy(index, device, part).wait_send()


def solution(mesh):
    n_gx, n_gy, n_gz = mesh.shape["gx"], mesh.shape["gy"], mesh.shape["gz"]

    def local(links, null_vectors, offsets, place):
        z_len, t_len, stencil, n_comp, width = links.shape[2:]
        n_vec = null_vectors.shape[4]
        q_count = z_len // 2
        aggregates = n_gy // 2 * q_count
        capacity = aggregates // 2
        peers = 2 * n_gy - 1
        lines = n_vec // 2
        dma = pltpu.SemaphoreType.DMA
        result = pl.pallas_call(
            functools.partial(kernel, (n_gx, n_gy, n_gz)),
            out_shape=jax.ShapeDtypeStruct((1, 1, stencil, capacity, 2 * n_vec * n_vec), BF16),
            in_specs=[
                pl.BlockSpec(memory_space=pltpu.HBM),
                pl.BlockSpec(memory_space=pltpu.HBM),
                pl.BlockSpec(memory_space=pltpu.SMEM),
                pl.BlockSpec(memory_space=pltpu.SMEM),
            ],
            out_specs=pl.BlockSpec(memory_space=pltpu.VMEM),
            scratch_shapes=[
                pltpu.VMEM((z_len, t_len, stencil, n_comp, width), BF16),
                pltpu.VMEM((z_len, t_len, n_vec, width), BF16),
                pltpu.VMEM((4, z_len, t_len, n_vec, width), BF16),
                pltpu.VMEM((2, t_len, n_vec, width), BF16),
                pltpu.VMEM((z_len + 2, t_len, width, width), BF16),
                pltpu.VMEM((z_len, t_len, n_vec, width), F32),
                pltpu.VMEM((q_count, 2 * n_vec, 4 * n_comp), BF16),
                pltpu.VMEM((q_count, 2 * n_vec, 4 * n_comp), BF16),
                pltpu.VMEM((q_count, 2 * n_vec, width), F32),
                pltpu.VMEM((PART, lines, width), F32),
                pltpu.VMEM((4, PART, lines, width), BF16),
                pltpu.VMEM((4, PART, lines, width), BF16),
                pltpu.VMEM((aggregates, ALL, lines, width), BF16),
                pltpu.VMEM((ALL * capacity * lines, width), F32),
                dma,
                dma,
                dma((4, 4)),
                dma((4, 4)),
                dma((2,)),
                dma((2,)),
                dma((2, 4)),
                dma((2, 4)),
                dma((2, peers)),
                dma((2, peers)),
            ],
            compiler_params=pltpu.CompilerParams(
                collective_id=0, has_side_effects=True, vmem_limit_bytes=63 * 2**20
            ),
            cost_estimate=pl.CostEstimate(
                flops=2 * z_len * t_len * stencil * n_comp * width * 6 * n_vec,
                bytes_accessed=links.size * 2 + null_vectors.size * 2,
                transcendentals=0,
            ),
        )(links, null_vectors, offsets.T, place.swapaxes(2, 3))
        return result.swapaxes(2, 3).astype(F32)

    placed = (
        P("gx", "gy", "gz", None, None, None, None),
        P("gx", "gy", "gz", None, None, None),
        P(),
        P(),
    )
    return jax.shard_map(
        local,
        mesh=mesh,
        in_specs=placed,
        out_specs=P("gx", "gz", None, None, None),
        check_vma=False,
    )
```

```python
import functools

import jax
import jax.numpy as jnp
from jax import lax
from jax.experimental import pallas as pl
from jax.experimental.pallas import tpu as pltpu
from jax.sharding import PartitionSpec as P

MESH = pl.DeviceIdType.MESH
F32 = jnp.float32
BF16 = jnp.bfloat16
ZT, ALL, PART = 4, 9, 7


def rotated(value):
    half = value.shape[-1] // 2
    return pltpu.roll(value, half, 1)


def right_blocks(vectors):
    value = vectors.astype(F32)
    half = value.shape[-1] // 2
    lane = lax.broadcasted_iota(jnp.int32, value.shape, 1)
    first = jnp.where(lane < half, value, -value)
    second = rotated(value)
    return jnp.concatenate([first, second, second, -first], 0).astype(BF16)


def hop(left, right):
    return lax.dot_general(
        left, right, (((1,), (1,)), ((), ())), preferred_element_type=F32
    ).astype(BF16)


def mm(left, right):
    return jnp.dot(left, right, preferred_element_type=F32)


def fold(product):
    rows = product.shape[0] // 4
    a, b, c, d = (product[i * rows : (i + 1) * rows] for i in range(4))
    lane = lax.broadcasted_iota(jnp.int32, a.shape, 1)
    return jnp.where(lane < a.shape[1] // 2, a + rotated(c), rotated(b) + d)


def kernel(
    sizes,
    links_hbm,
    vec_hbm,
    offsets_ref,
    place_ref,
    out_ref,
    links,
    vec,
    halo,
    halo_z,
    blocks,
    vec32,
    left,
    left_t,
    acc,
    own,
    sendbuf,
    arrived,
    gathered,
    flat,
    link_sem,
    vec_sem,
    hs_sem,
    hr_sem,
    zs_sem,
    zr_sem,
    rs_sem,
    rr_sem,
    gs_sem,
    gr_sem,
):
    n_gx, n_gy, n_gz = sizes
    z_len, t_len, n_vec = vec.shape[0], vec.shape[1], vec.shape[2]
    n_comp = links.shape[3]
    q_count = z_len // 2
    gx, gy, gz = lax.axis_index("gx"), lax.axis_index("gy"), lax.axis_index("gz")
    xb, yb = gx % 2, gy % 2
    x_out = (gx + 2 * xb - 1 + n_gx) % n_gx
    x_in = gx + 1 - 2 * xb
    y_out = (gy + 2 * yb - 1 + n_gy) % n_gy
    y_in = gy + 1 - 2 * yb
    z_up, z_down = (gz + 1) % n_gz, (gz + n_gz - 1) % n_gz

    peers = []
    for dx in range(2):
        for dy in range(n_gy):
            if dx or dy:
                peers.append((dx, dy, (gx + dx * (1 - 2 * xb), (gy + dy) % n_gy, gz)))

    barrier = pltpu.get_barrier_semaphore()
    for _, _, device in peers:
        pl.semaphore_signal(barrier, inc=1, device_id=device, device_id_type=MESH)
    for device in ((x_out, gy, gz), (gx, gy, z_up), (gx, gy, z_down)):
        pl.semaphore_signal(barrier, inc=1, device_id=device, device_id_type=MESH)

    vec_copy = pltpu.make_async_copy(vec_hbm.at[0, 0], vec, vec_sem)
    vec_copy.start()

    def square(d):
        return (xb + d % 2) % 2 + 2 * ((yb + d // 2) % 2)

    link_copy = pltpu.make_async_copy(links_hbm.at[0, 0], links, link_sem)
    link_copy.start()

    codes = [
        offsets_ref[0, k] + 3 * offsets_ref[1, k] + 9 * offsets_ref[2, k] + 27 * offsets_ref[3, k]
        for k in range(ALL)
    ]

    def position(code):
        found = jnp.int32(0)
        for k in range(1, ALL):
            found = jnp.where(codes[k] == code, k, found)
        return found

    x_sign, y_sign = 2 * xb - 1, 2 * yb - 1
    k_zero = position(0)
    k_zp, k_zm, k_tp, k_tm = position(9), position(-9), position(27), position(-27)
    k_dirs = (position(-x_sign), position(x_sign), position(-3 * y_sign), position(3 * y_sign))

    vec_copy.wait()
    pl.semaphore_wait(barrier, len(peers) + 3)

    up_copy = pltpu.make_async_remote_copy(
        src_ref=vec.at[z_len - 1],
        dst_ref=halo_z.at[0],
        send_sem=zs_sem.at[0],
        recv_sem=zr_sem.at[0],
        device_id=(gx, gy, z_up),
        device_id_type=MESH,
    )
    down_copy = pltpu.make_async_remote_copy(
        src_ref=vec.at[0],
        dst_ref=halo_z.at[1],
        send_sem=zs_sem.at[1],
        recv_sem=zr_sem.at[1],
        device_id=(gx, gy, z_down),
        device_id_type=MESH,
    )
    up_copy.start()
    down_copy.start()

    targets = ((x_in, gy, gz), (x_out, gy, gz), (gx, y_in, gz), (gx, y_out, gz))

    def halo_copy(direction, d):
        flip = 1 if direction < 2 else 2
        if flip == 1:
            q = (xb + 1 + d % 2) % 2 + 2 * ((yb + d // 2) % 2)
        else:
            q = (xb + d % 2) % 2 + 2 * ((yb + 1 + d // 2) % 2)
        rows = pl.ds(2 * q, 2)
        return pltpu.make_async_remote_copy(
            src_ref=vec.at[rows],
            dst_ref=halo.at[direction, rows],
            send_sem=hs_sem.at[direction, d],
            recv_sem=hr_sem.at[direction, d],
            device_id=targets[direction],
            device_id_type=MESH,
        )

    def halo_arrival(direction, d):
        rows = pl.ds(2 * square(d), 2)
        return pltpu.make_async_remote_copy(
            src_ref=vec.at[rows],
            dst_ref=halo.at[direction, rows],
            send_sem=hs_sem.at[direction, d],
            recv_sem=hr_sem.at[direction, d],
            device_id=targets[direction],
            device_id_type=MESH,
        )

    for d in (1, 2, 3, 0):
        for direction in (1, 3, 0, 2):
            halo_copy(direction, d).start()

    def prepare(z, carry):
        for t in range(t_len):
            blocks[z + 1, t] = right_blocks(vec[z, t])
            vec32[z, t] = vec[z, t].astype(F32)
        return carry

    lax.fori_loop(0, z_len, prepare, 0)

    def prepare_left(q, carry):
        def pieces(dz, t):
            return [vec32[2 * q + dz, t, pl.ds(s, n_vec // 2, stride=2), :] for s in range(2)]

        site = {(dz, t): pieces(dz, t) for dz in range(2) for t in range(2)}
        shape = site[0, 0][0].shape
        lane = lax.broadcasted_iota(jnp.int32, shape, 1)
        low = lane < n_comp

        def pair(one, two):
            real = [jnp.where(low, one[s], rotated(two[s])) for s in range(2)]
            imag = [jnp.where(low, rotated(one[s]), two[s]) for s in range(2)]
            return jnp.concatenate(real + imag, 0).astype(BF16)

        left[q, :, : 2 * n_comp] = pair(site[0, 0], site[0, 1])
        left[q, :, 2 * n_comp :] = pair(site[1, 0], site[1, 1])
        left_t[q, :, : 2 * n_comp] = pair(site[0, 0], site[1, 0])
        left_t[q, :, 2 * n_comp :] = pair(site[0, 1], site[1, 1])
        return carry

    lax.fori_loop(0, q_count, prepare_left, 0)

    up_copy.wait_recv()
    down_copy.wait_recv()
    for t in range(t_len):
        blocks[0, t] = right_blocks(halo_z[0, t])
        blocks[z_len + 1, t] = right_blocks(halo_z[1, t])

    def rs_copy(d, part):
        rows = pl.ds(0, ZT) if part == 0 else pl.ds(ZT, PART - ZT)
        dx, dy = d % 2, d // 2
        return pltpu.make_async_remote_copy(
            src_ref=sendbuf.at[d, rows],
            dst_ref=arrived.at[d, rows],
            send_sem=rs_sem.at[part, d],
            recv_sem=rr_sem.at[part, d],
            device_id=(gx + dx * (1 - 2 * xb), gy + dy * (1 - 2 * yb), gz),
            device_id_type=MESH,
        )

    def local_part(d, put):
        q = square(d)
        z0 = 2 * q
        zero, z_inner, z_outer, t_inner, t_outer = {}, {}, {}, {}, {}
        for dz in range(2):
            z = z0 + dz
            k_in, k_back = (k_zm, k_zp) if dz == 0 else (k_zp, k_zm)
            for t in range(2):
                lhs = jnp.concatenate(
                    [
                        links[z, t, k_zero],
                        links[z0 + 1 - dz, t, k_in],
                        links[z, 1 - t, k_tp],
                        links[z, 1 - t, k_tm],
                    ],
                    0,
                )
                res = hop(lhs, blocks[z + 1, t])
                rows = [res[i * n_comp : (i + 1) * n_comp] for i in range(4)]
                zero[dz, t] = rows[0]
                z_inner[1 - dz, t] = rows[1]
                t_inner[dz, 1 - t] = rows[2] if t == 1 else rows[3]
                t_outer[dz, 1 - t] = rows[3] if t == 1 else rows[2]
                edge = blocks[z0, t] if dz == 0 else blocks[z0 + 3, t]
                z_outer[dz, t] = hop(links[z, t, k_in], edge)
        order = ((0, 0), (0, 1), (1, 0), (1, 1))
        lq = left[q]
        lt = left_t[q]
        total = mm(lq, jnp.concatenate([zero[s] for s in order], 0))
        total = total + mm(lq, jnp.concatenate([z_inner[s] for s in order], 0))
        total = total + mm(lq, jnp.concatenate([t_inner[s] for s in order], 0))
        acc[q] = total
        half = 2 * n_comp
        put(0, fold(mm(lq[:, half:], jnp.concatenate([z_outer[1, 0], z_outer[1, 1]], 0))))
        put(1, fold(mm(lq[:, :half], jnp.concatenate([z_outer[0, 0], z_outer[0, 1]], 0))))
        put(2, fold(mm(lt[:, half:], jnp.concatenate([t_outer[0, 1], t_outer[1, 1]], 0))))
        put(3, fold(mm(lt[:, :half], jnp.concatenate([t_outer[0, 0], t_outer[1, 0]], 0))))

    def halo_part(d, put):
        q = square(d)
        z0 = 2 * q
        lq = left[q]
        sums = []
        for direction in range(4):
            halo_arrival(direction, d).wait_recv()
            rows = []
            for dz in range(2):
                for t in range(2):
                    rows.append(
                        hop(
                            links[z0 + dz, t, k_dirs[direction]],
                            right_blocks(halo[direction, z0 + dz, t]),
                        )
                    )
            sums.append(mm(lq, jnp.concatenate(rows, 0)))
        put(4, fold(acc[q] + sums[0] + sums[2]))
        put(5, fold(sums[1]))
        put(6, fold(sums[3]))

    def put_own(i, value):
        own[i] = value

    def local_step(d, carry):
        def put(i, value):
            sendbuf[d, i] = value.astype(BF16)

        local_part(d, put)
        rs_copy(d, 0).start()
        return carry

    def halo_step(d, carry):
        def put(i, value):
            sendbuf[d, i] = value.astype(BF16)

        halo_part(d, put)
        rs_copy(d, 1).start()
        return carry

    link_copy.wait()
    lax.fori_loop(1, 4, local_step, 0)
    local_part(0, put_own)
    lax.fori_loop(1, 4, halo_step, 0)

    mine = gy // 2 * q_count + square(0)

    def ag_copy(index, device, part):
        rows = pl.ds(0, ZT) if part == 0 else pl.ds(ZT, ALL - ZT)
        return pltpu.make_async_remote_copy(
            src_ref=gathered.at[mine, rows],
            dst_ref=gathered.at[mine, rows],
            send_sem=gs_sem.at[part, index],
            recv_sem=gr_sem.at[part, index],
            device_id=device,
            device_id_type=MESH,
        )

    def put_all(i, value):
        gathered[mine, i] = value.astype(BF16)

    def got(d, i):
        return arrived[d, i].astype(F32)

    for d in range(1, 4):
        rs_copy(d, 0).wait_recv()
    for i in range(ZT):
        put_all(i, own[i] + got(1, i) + got(2, i) + got(3, i))
    for index, (_, _, device) in enumerate(peers):
        ag_copy(index, device, 0).start()

    halo_part(0, put_own)

    for d in range(1, 4):
        rs_copy(d, 1).wait_recv()
    put_all(4, own[4] + got(1, 4) + got(2, 4) + got(3, 4))
    put_all(6 - xb, own[5] + got(2, 5))
    put_all(5 + xb, got(1, 5) + got(3, 5))
    put_all(8 - yb, own[6] + got(1, 6))
    put_all(7 + yb, got(2, 6) + got(3, 6))
    for index, (_, _, device) in enumerate(peers):
        ag_copy(index, device, 1).start()

    kinds = []
    for k in range(ALL):
        kind = jnp.int32(0)
        for i, code in enumerate((9, -9, 27, -27, 0, 1, -1, 3, -3)):
            if i:
                kind = jnp.where(codes[k] == code, i, kind)
        kinds.append(kind)
    capacity = out_ref.shape[3]
    cy_count = n_gy // 2

    up_copy.wait_send()
    down_copy.wait_send()
    for d in range(4):
        for direction in range(4):
            halo_copy(direction, d).wait_send()
    for d in range(1, 4):
        for part in range(2):
            rs_copy(d, part).wait_send()
    for part in range(2):
        for index, (_, _, device) in enumerate(peers):
            ag_copy(index, device, part).wait_recv()

    lines = n_vec // 2

    sources = []
    for slot in range(capacity):
        source = jnp.int32(0)
        for cy in range(cy_count):
            for q in range(q_count):
                here = place_ref[gx // 2, cy, 0, gz * q_count + q]
                source = jnp.where(here == xb * capacity + slot, cy * q_count + q, source)
        sources.append(source)
    for k in range(ALL):
        base = k * capacity * lines
        for slot in range(capacity):
            at = base + slot * lines
            flat[at : at + lines, :] = gathered[sources[slot], kinds[k]].astype(F32)
        for i in range(lines):
            out_ref[0, 0, k, :, 2 * n_comp * i : 2 * n_comp * (i + 1)] = flat[
                pl.ds(base + i, capacity, stride=lines), :
            ].astype(BF16)
    for part in range(2):
        for index, (_, _, device) in enumerate(peers):
            ag_copy(index, device, part).wait_send()


def solution(mesh):
    n_gx, n_gy, n_gz = mesh.shape["gx"], mesh.shape["gy"], mesh.shape["gz"]

    def local(links, null_vectors, offsets, place):
        z_len, t_len, stencil, n_comp, width = links.shape[2:]
        n_vec = null_vectors.shape[4]
        q_count = z_len // 2
        aggregates = n_gy // 2 * q_count
        capacity = aggregates // 2
        peers = 2 * n_gy - 1
        lines = n_vec // 2
        dma = pltpu.SemaphoreType.DMA
        result = pl.pallas_call(
            functools.partial(kernel, (n_gx, n_gy, n_gz)),
            out_shape=jax.ShapeDtypeStruct((1, 1, stencil, capacity, 2 * n_vec * n_vec), BF16),
            in_specs=[
                pl.BlockSpec(memory_space=pltpu.HBM),
                pl.BlockSpec(memory_space=pltpu.HBM),
                pl.BlockSpec(memory_space=pltpu.SMEM),
                pl.BlockSpec(memory_space=pltpu.SMEM),
            ],
            out_specs=pl.BlockSpec(memory_space=pltpu.VMEM),
            scratch_shapes=[
                pltpu.VMEM((z_len, t_len, stencil, n_comp, width), BF16),
                pltpu.VMEM((z_len, t_len, n_vec, width), BF16),
                pltpu.VMEM((4, z_len, t_len, n_vec, width), BF16),
                pltpu.VMEM((2, t_len, n_vec, width), BF16),
                pltpu.VMEM((z_len + 2, t_len, width, width), BF16),
                pltpu.VMEM((z_len, t_len, n_vec, width), F32),
                pltpu.VMEM((q_count, 2 * n_vec, 4 * n_comp), BF16),
                pltpu.VMEM((q_count, 2 * n_vec, 4 * n_comp), BF16),
                pltpu.VMEM((q_count, 2 * n_vec, width), F32),
                pltpu.VMEM((PART, lines, width), F32),
                pltpu.VMEM((4, PART, lines, width), BF16),
                pltpu.VMEM((4, PART, lines, width), BF16),
                pltpu.VMEM((aggregates, ALL, lines, width), BF16),
                pltpu.VMEM((ALL * capacity * lines, width), F32),
                dma,
                dma,
                dma((4, 4)),
                dma((4, 4)),
                dma((2,)),
                dma((2,)),
                dma((2, 4)),
                dma((2, 4)),
                dma((2, peers)),
                dma((2, peers)),
            ],
            compiler_params=pltpu.CompilerParams(
                collective_id=0, has_side_effects=True, vmem_limit_bytes=63 * 2**20
            ),
            cost_estimate=pl.CostEstimate(
                flops=2 * z_len * t_len * stencil * n_comp * width * 6 * n_vec,
                bytes_accessed=links.size * 2 + null_vectors.size * 2,
                transcendentals=0,
            ),
        )(links, null_vectors, offsets.T, place.swapaxes(2, 3))
        return result.swapaxes(2, 3).astype(F32)

    placed = (
        P("gx", "gy", "gz", None, None, None, None),
        P("gx", "gy", "gz", None, None, None),
        P(),
        P(),
    )
    return jax.shard_map(
        local,
        mesh=mesh,
        in_specs=placed,
        out_specs=P("gx", "gz", None, None, None),
        check_vma=False,
    )
```

```python
import functools

import jax
import jax.numpy as jnp
from jax import lax
from jax.experimental import pallas as pl
from jax.experimental.pallas import tpu as pltpu
from jax.sharding import PartitionSpec as P

MESH = pl.DeviceIdType.MESH
F32 = jnp.float32
BF16 = jnp.bfloat16
ZT, ALL, PART = 4, 9, 7


def rotated(value):
    half = value.shape[-1] // 2
    return pltpu.roll(value, half, 1)


def right_blocks(vectors):
    value = vectors.astype(F32)
    half = value.shape[-1] // 2
    lane = lax.broadcasted_iota(jnp.int32, value.shape, 1)
    first = jnp.where(lane < half, value, -value)
    second = rotated(value)
    return jnp.concatenate([first, second, second, -first], 0).astype(BF16)


def hop(left, right):
    return lax.dot_general(
        left, right, (((1,), (1,)), ((), ())), preferred_element_type=F32
    ).astype(BF16)


def mm(left, right):
    return jnp.dot(left, right, preferred_element_type=F32)


def fold(product):
    rows = product.shape[0] // 4
    a, b, c, d = (product[i * rows : (i + 1) * rows] for i in range(4))
    lane = lax.broadcasted_iota(jnp.int32, a.shape, 1)
    return jnp.where(lane < a.shape[1] // 2, a + rotated(c), rotated(b) + d)


def kernel(
    sizes,
    links_hbm,
    vec_hbm,
    offsets_ref,
    place_ref,
    out_ref,
    links,
    vec,
    halo,
    halo_z,
    blocks,
    vec32,
    left,
    left_t,
    acc,
    own,
    sendbuf,
    arrived,
    gathered,
    flat,
    link_sem,
    vec_sem,
    hs_sem,
    hr_sem,
    zs_sem,
    zr_sem,
    rs_sem,
    rr_sem,
    gs_sem,
    gr_sem,
):
    n_gx, n_gy, n_gz = sizes
    z_len, t_len, n_vec = vec.shape[0], vec.shape[1], vec.shape[2]
    n_comp = links.shape[3]
    q_count = z_len // 2
    gx, gy, gz = lax.axis_index("gx"), lax.axis_index("gy"), lax.axis_index("gz")
    xb, yb = gx % 2, gy % 2
    x_out = (gx + 2 * xb - 1 + n_gx) % n_gx
    x_in = gx + 1 - 2 * xb
    y_out = (gy + 2 * yb - 1 + n_gy) % n_gy
    y_in = gy + 1 - 2 * yb
    z_up, z_down = (gz + 1) % n_gz, (gz + n_gz - 1) % n_gz

    peers = []
    for dx in range(2):
        for dy in range(n_gy):
            if dx or dy:
                peers.append((dx, dy, (gx + dx * (1 - 2 * xb), (gy + dy) % n_gy, gz)))

    peers.sort(key=lambda peer: -(peer[0] + min(peer[1], n_gy - peer[1])))

    barrier = pltpu.get_barrier_semaphore()
    for _, _, device in peers:
        pl.semaphore_signal(barrier, inc=1, device_id=device, device_id_type=MESH)
    for device in ((x_out, gy, gz), (gx, gy, z_up), (gx, gy, z_down)):
        pl.semaphore_signal(barrier, inc=1, device_id=device, device_id_type=MESH)

    vec_copy = pltpu.make_async_copy(vec_hbm.at[0, 0], vec, vec_sem)
    vec_copy.start()

    def square(d):
        return (xb + d % 2) % 2 + 2 * ((yb + d // 2) % 2)

    link_copy = pltpu.make_async_copy(links_hbm.at[0, 0], links, link_sem)
    link_copy.start()

    codes = [
        offsets_ref[0, k] + 3 * offsets_ref[1, k] + 9 * offsets_ref[2, k] + 27 * offsets_ref[3, k]
        for k in range(ALL)
    ]

    def position(code):
        found = jnp.int32(0)
        for k in range(1, ALL):
            found = jnp.where(codes[k] == code, k, found)
        return found

    x_sign, y_sign = 2 * xb - 1, 2 * yb - 1
    k_zero = position(0)
    k_zp, k_zm, k_tp, k_tm = position(9), position(-9), position(27), position(-27)
    k_dirs = (position(-x_sign), position(x_sign), position(-3 * y_sign), position(3 * y_sign))

    vec_copy.wait()
    pl.semaphore_wait(barrier, len(peers) + 3)

    up_copy = pltpu.make_async_remote_copy(
        src_ref=vec.at[z_len - 1],
        dst_ref=halo_z.at[0],
        send_sem=zs_sem.at[0],
        recv_sem=zr_sem.at[0],
        device_id=(gx, gy, z_up),
        device_id_type=MESH,
    )
    down_copy = pltpu.make_async_remote_copy(
        src_ref=vec.at[0],
        dst_ref=halo_z.at[1],
        send_sem=zs_sem.at[1],
        recv_sem=zr_sem.at[1],
        device_id=(gx, gy, z_down),
        device_id_type=MESH,
    )
    up_copy.start()
    down_copy.start()

    targets = ((x_in, gy, gz), (x_out, gy, gz), (gx, y_in, gz), (gx, y_out, gz))

    def halo_copy(direction, d):
        flip = 1 if direction < 2 else 2
        if flip == 1:
            q = (xb + 1 + d % 2) % 2 + 2 * ((yb + d // 2) % 2)
        else:
            q = (xb + d % 2) % 2 + 2 * ((yb + 1 + d // 2) % 2)
        rows = pl.ds(2 * q, 2)
        return pltpu.make_async_remote_copy(
            src_ref=vec.at[rows],
            dst_ref=halo.at[direction, rows],
            send_sem=hs_sem.at[direction, d],
            recv_sem=hr_sem.at[direction, d],
            device_id=targets[direction],
            device_id_type=MESH,
        )

    def halo_arrival(direction, d):
        rows = pl.ds(2 * square(d), 2)
        return pltpu.make_async_remote_copy(
            src_ref=vec.at[rows],
            dst_ref=halo.at[direction, rows],
            send_sem=hs_sem.at[direction, d],
            recv_sem=hr_sem.at[direction, d],
            device_id=targets[direction],
            device_id_type=MESH,
        )

    for d in (3, 2, 1, 0):
        for direction in (1, 3, 0, 2):
            halo_copy(direction, d).start()

    def prepare(z, carry):
        for t in range(t_len):
            blocks[z + 1, t] = right_blocks(vec[z, t])
            vec32[z, t] = vec[z, t].astype(F32)
        return carry

    lax.fori_loop(0, z_len, prepare, 0)

    def prepare_left(q, carry):
        def pieces(dz, t):
            return [vec32[2 * q + dz, t, pl.ds(s, n_vec // 2, stride=2), :] for s in range(2)]

        site = {(dz, t): pieces(dz, t) for dz in range(2) for t in range(2)}
        shape = site[0, 0][0].shape
        lane = lax.broadcasted_iota(jnp.int32, shape, 1)
        low = lane < n_comp

        def pair(one, two):
            real = [jnp.where(low, one[s], rotated(two[s])) for s in range(2)]
            imag = [jnp.where(low, rotated(one[s]), two[s]) for s in range(2)]
            return jnp.concatenate(real + imag, 0).astype(BF16)

        left[q, :, : 2 * n_comp] = pair(site[0, 0], site[0, 1])
        left[q, :, 2 * n_comp :] = pair(site[1, 0], site[1, 1])
        left_t[q, :, : 2 * n_comp] = pair(site[0, 0], site[1, 0])
        left_t[q, :, 2 * n_comp :] = pair(site[0, 1], site[1, 1])
        return carry

    lax.fori_loop(0, q_count, prepare_left, 0)

    up_copy.wait_recv()
    down_copy.wait_recv()
    for t in range(t_len):
        blocks[0, t] = right_blocks(halo_z[0, t])
        blocks[z_len + 1, t] = right_blocks(halo_z[1, t])

    def rs_copy(d, part):
        rows = pl.ds(0, ZT) if part == 0 else pl.ds(ZT, PART - ZT)
        dx, dy = d % 2, d // 2
        return pltpu.make_async_remote_copy(
            src_ref=sendbuf.at[d, rows],
            dst_ref=arrived.at[d, rows],
            send_sem=rs_sem.at[part, d],
            recv_sem=rr_sem.at[part, d],
            device_id=(gx + dx * (1 - 2 * xb), gy + dy * (1 - 2 * yb), gz),
            device_id_type=MESH,
        )

    def local_part(d, put):
        q = square(d)
        z0 = 2 * q
        zero, z_inner, z_outer, t_inner, t_outer = {}, {}, {}, {}, {}
        for dz in range(2):
            z = z0 + dz
            k_in, k_back = (k_zm, k_zp) if dz == 0 else (k_zp, k_zm)
            for t in range(2):
                lhs = jnp.concatenate(
                    [
                        links[z, t, k_zero],
                        links[z0 + 1 - dz, t, k_in],
                        links[z, 1 - t, k_tp],
                        links[z, 1 - t, k_tm],
                    ],
                    0,
                )
                res = hop(lhs, blocks[z + 1, t])
                rows = [res[i * n_comp : (i + 1) * n_comp] for i in range(4)]
                zero[dz, t] = rows[0]
                z_inner[1 - dz, t] = rows[1]
                t_inner[dz, 1 - t] = rows[2] if t == 1 else rows[3]
                t_outer[dz, 1 - t] = rows[3] if t == 1 else rows[2]
                edge = blocks[z0, t] if dz == 0 else blocks[z0 + 3, t]
                z_outer[dz, t] = hop(links[z, t, k_in], edge)
        order = ((0, 0), (0, 1), (1, 0), (1, 1))
        lq = left[q]
        lt = left_t[q]
        total = mm(lq, jnp.concatenate([zero[s] for s in order], 0))
        total = total + mm(lq, jnp.concatenate([z_inner[s] for s in order], 0))
        total = total + mm(lq, jnp.concatenate([t_inner[s] for s in order], 0))
        acc[q] = total
        half = 2 * n_comp
        put(0, fold(mm(lq[:, half:], jnp.concatenate([z_outer[1, 0], z_outer[1, 1]], 0))))
        put(1, fold(mm(lq[:, :half], jnp.concatenate([z_outer[0, 0], z_outer[0, 1]], 0))))
        put(2, fold(mm(lt[:, half:], jnp.concatenate([t_outer[0, 1], t_outer[1, 1]], 0))))
        put(3, fold(mm(lt[:, :half], jnp.concatenate([t_outer[0, 0], t_outer[1, 0]], 0))))

    def halo_part(d, put):
        q = square(d)
        z0 = 2 * q
        lq = left[q]
        sums = []
        for direction in range(4):
            halo_arrival(direction, d).wait_recv()
            rows = []
            for dz in range(2):
                for t in range(2):
                    rows.append(
                        hop(
                            links[z0 + dz, t, k_dirs[direction]],
                            right_blocks(halo[direction, z0 + dz, t]),
                        )
                    )
            sums.append(mm(lq, jnp.concatenate(rows, 0)))
        put(4, fold(acc[q] + sums[0] + sums[2]))
        put(5, fold(sums[1]))
        put(6, fold(sums[3]))

    def put_own(i, value):
        own[i] = value

    def local_step(step, carry):
        d = 4 - step

        def put(i, value):
            sendbuf[d, i] = value.astype(BF16)

        local_part(d, put)
        rs_copy(d, 0).start()
        return carry

    def halo_step(step, carry):
        d = 4 - step

        def put(i, value):
            sendbuf[d, i] = value.astype(BF16)

        halo_part(d, put)
        rs_copy(d, 1).start()
        return carry

    link_copy.wait()
    lax.fori_loop(1, 4, local_step, 0)
    local_part(0, put_own)
    lax.fori_loop(1, 4, halo_step, 0)

    mine = gy // 2 * q_count + square(0)

    def ag_copy(index, device, part):
        rows = pl.ds(0, ZT) if part == 0 else pl.ds(ZT, ALL - ZT)
        return pltpu.make_async_remote_copy(
            src_ref=gathered.at[mine, rows],
            dst_ref=gathered.at[mine, rows],
            send_sem=gs_sem.at[part, index],
            recv_sem=gr_sem.at[part, index],
            device_id=device,
            device_id_type=MESH,
        )

    def put_all(i, value):
        gathered[mine, i] = value.astype(BF16)

    def got(d, i):
        return arrived[d, i].astype(F32)

    for d in range(1, 4):
        rs_copy(d, 0).wait_recv()
    for i in range(ZT):
        put_all(i, own[i] + got(1, i) + got(2, i) + got(3, i))
    for index, (_, _, device) in enumerate(peers):
        ag_copy(index, device, 0).start()

    halo_part(0, put_own)

    for d in range(1, 4):
        rs_copy(d, 1).wait_recv()
    put_all(4, own[4] + got(1, 4) + got(2, 4) + got(3, 4))
    put_all(6 - xb, own[5] + got(2, 5))
    put_all(5 + xb, got(1, 5) + got(3, 5))
    put_all(8 - yb, own[6] + got(1, 6))
    put_all(7 + yb, got(2, 6) + got(3, 6))
    for index, (_, _, device) in enumerate(peers):
        ag_copy(index, device, 1).start()

    kinds = []
    for k in range(ALL):
        kind = jnp.int32(0)
        for i, code in enumerate((9, -9, 27, -27, 0, 1, -1, 3, -3)):
            if i:
                kind = jnp.where(codes[k] == code, i, kind)
        kinds.append(kind)
    capacity = out_ref.shape[3]
    cy_count = n_gy // 2

    up_copy.wait_send()
    down_copy.wait_send()
    for d in range(4):
        for direction in range(4):
            halo_copy(direction, d).wait_send()
    for d in range(1, 4):
        for part in range(2):
            rs_copy(d, part).wait_send()
    for part in range(2):
        for index, (_, _, device) in enumerate(peers):
            ag_copy(index, device, part).wait_recv()

    lines = n_vec // 2

    sources = []
    for slot in range(capacity):
        source = jnp.int32(0)
        for cy in range(cy_count):
            for q in range(q_count):
                here = place_ref[gx // 2, cy, 0, gz * q_count + q]
                source = jnp.where(here == xb * capacity + slot, cy * q_count + q, source)
        sources.append(source)
    for k in range(ALL):
        base = k * capacity * lines
        for slot in range(capacity):
            at = base + slot * lines
            flat[at : at + lines, :] = gathered[sources[slot], kinds[k]].astype(F32)
        for i in range(lines):
            out_ref[0, 0, k, :, 2 * n_comp * i : 2 * n_comp * (i + 1)] = flat[
                pl.ds(base + i, capacity, stride=lines), :
            ].astype(BF16)
    for part in range(2):
        for index, (_, _, device) in enumerate(peers):
            ag_copy(index, device, part).wait_send()


def solution(mesh):
    n_gx, n_gy, n_gz = mesh.shape["gx"], mesh.shape["gy"], mesh.shape["gz"]

    def local(links, null_vectors, offsets, place):
        z_len, t_len, stencil, n_comp, width = links.shape[2:]
        n_vec = null_vectors.shape[4]
        q_count = z_len // 2
        aggregates = n_gy // 2 * q_count
        capacity = aggregates // 2
        peers = 2 * n_gy - 1
        lines = n_vec // 2
        dma = pltpu.SemaphoreType.DMA
        result = pl.pallas_call(
            functools.partial(kernel, (n_gx, n_gy, n_gz)),
            out_shape=jax.ShapeDtypeStruct((1, 1, stencil, capacity, 2 * n_vec * n_vec), BF16),
            in_specs=[
                pl.BlockSpec(memory_space=pltpu.HBM),
                pl.BlockSpec(memory_space=pltpu.HBM),
                pl.BlockSpec(memory_space=pltpu.SMEM),
                pl.BlockSpec(memory_space=pltpu.SMEM),
            ],
            out_specs=pl.BlockSpec(memory_space=pltpu.VMEM),
            scratch_shapes=[
                pltpu.VMEM((z_len, t_len, stencil, n_comp, width), BF16),
                pltpu.VMEM((z_len, t_len, n_vec, width), BF16),
                pltpu.VMEM((4, z_len, t_len, n_vec, width), BF16),
                pltpu.VMEM((2, t_len, n_vec, width), BF16),
                pltpu.VMEM((z_len + 2, t_len, width, width), BF16),
                pltpu.VMEM((z_len, t_len, n_vec, width), F32),
                pltpu.VMEM((q_count, 2 * n_vec, 4 * n_comp), BF16),
                pltpu.VMEM((q_count, 2 * n_vec, 4 * n_comp), BF16),
                pltpu.VMEM((q_count, 2 * n_vec, width), F32),
                pltpu.VMEM((PART, lines, width), F32),
                pltpu.VMEM((4, PART, lines, width), BF16),
                pltpu.VMEM((4, PART, lines, width), BF16),
                pltpu.VMEM((aggregates, ALL, lines, width), BF16),
                pltpu.VMEM((ALL * capacity * lines, width), F32),
                dma,
                dma,
                dma((4, 4)),
                dma((4, 4)),
                dma((2,)),
                dma((2,)),
                dma((2, 4)),
                dma((2, 4)),
                dma((2, peers)),
                dma((2, peers)),
            ],
            compiler_params=pltpu.CompilerParams(
                collective_id=0, has_side_effects=True, vmem_limit_bytes=63 * 2**20
            ),
            cost_estimate=pl.CostEstimate(
                flops=2 * z_len * t_len * stencil * n_comp * width * 6 * n_vec,
                bytes_accessed=links.size * 2 + null_vectors.size * 2,
                transcendentals=0,
            ),
        )(links, null_vectors, offsets.T, place.swapaxes(2, 3))
        return result.swapaxes(2, 3).astype(F32)

    placed = (
        P("gx", "gy", "gz", None, None, None, None),
        P("gx", "gy", "gz", None, None, None),
        P(),
        P(),
    )
    return jax.shard_map(
        local,
        mesh=mesh,
        in_specs=placed,
        out_specs=P("gx", "gz", None, None, None),
        check_vma=False,
    )
```
